32 devices in a mesh: dp: 16 (over z, x, core), code: 2 (over y).
Axes of the slice: x: 2, y: 2, z: 4, core: 2. Of those that a mesh axis runs over, the one named last changes fastest.
Arguments:
- items: float32 [4096, 512], P(('dp', 'code')), may hold values from -6 to 6
- codewords: float32 [8192, 512], P('code'), may hold values from -6 to 6
- assign: int32 [4096], P('dp'), may hold values from 0 to 8191, as said below
Outputs:
- new_codewords: float32 [8192, 512], P('code', 'dp')
- residual: float32 [4096, 512], P(('dp', 'code'))
The draws below stay inside these ranges and needn't reach their ends.
Inputs may be any that keep to these rules, and one draw needn't show every extreme that they name: `assign`: the items are laid out in aligned blocks of 128 (the items of one device). Splitting the codewords into equal ranges, one per index of code, the items of one block name codewords of exactly half of the ranges, 128 items for each such range.
All inputs are finite; a program needn't handle non-finite values.
Results may differ from the reference program's by a relative error of at most 0.0003.
Values sent between devices are 32-bit elements; how exact they have to be, the bound alone decides.
A program may use at most 64 MiB of HBM per device.

```python
import math
import jax
import jax.numpy as jnp
from jax import lax

D = 512
K = 8192
ROWS_DEV = 128
ITERS = 3
ITEMS = 4096
HALF_GRP = 64
N_CODE = 2


def one_block(block_key):
    first_key, second_key, third_key = jax.random.split(block_key, 3)
    ranges = jax.random.permutation(first_key, jnp.arange(N_CODE, dtype=jnp.int32))
    owner_half = ranges[jnp.arange(N_CODE, dtype=jnp.int32) // 2]
    owner_rows = jnp.repeat(owner_half, HALF_GRP)
    owner_rows = jax.random.permutation(second_key, owner_rows)
    within = jax.random.randint(third_key, (ROWS_DEV,), 0, K // N_CODE, dtype=jnp.int32)
    return owner_rows * (K // N_CODE) + within


def draw_assign(key, part):
    block_keys = jax.random.split(jax.random.fold_in(key, 17), ITEMS // ROWS_DEV)
    return jax.vmap(one_block)(block_keys).reshape(ITEMS).astype(jnp.int32)


def block_scale(key, dims, cuts, low, high):
    factor_of, own = 1.0, jax.random.fold_in(key, 6)
    for position, shards_of in cuts:
        draws = jnp.exp(jax.random.uniform(jax.random.fold_in(own, position), (shards_of,), jnp.float32, low / len(cuts), high / len(cuts)))
        factor_of = factor_of * jnp.repeat(draws, dims[position] // shards_of).reshape([-1 if axis == position else 1 for axis in range(len(dims))])
    return factor_of


def bell_draw(stream_key, extent, spread, most, cuts=(), kind=jnp.bfloat16):
    gain = block_scale(stream_key, extent, cuts, -0.22, 0.18) if cuts else 1.0
    drawn = jax.random.normal(stream_key, extent, jnp.float32) * spread * gain
    return jnp.minimum(jnp.maximum(drawn, -most), most).astype(kind)


def setup_inputs(seed: int = 0) -> dict:
    keys = jax.random.split(jax.random.key(seed), 4)
    items = bell_draw(keys[0], (ITEMS, D), 1.0, 6.0, ((0, 32),), jnp.float32)
    codewords = bell_draw(keys[1], (K, D), 1.0, 6.0, ((0, 2),), jnp.float32)
    assign = draw_assign(jax.random.fold_in(keys[3], 71), 0)
    return {"items": items, "codewords": codewords, "assign": assign}


epsilon = 1e-05
inverse_temp = 64.0

def unit_rows(values):
    return values * lax.rsqrt(lax.optimization_barrier(jnp.mean(values * values, axis=-1, keepdims=True)) + epsilon)

def reference(items, codewords, assign):
    scaled = unit_rows(codewords) * (inverse_temp / D)
    block = math.gcd(ITEMS, 1024)
    item_blocks = items.reshape(ITEMS // block, block, D)

    def kernel_of(rows_block):
        return jnp.exp(jnp.dot(unit_rows(rows_block), scaled.T, precision=lax.Precision.HIGHEST, preferred_element_type=jnp.float32))

    def first_sweep(col_acc, rows_block):
        return (col_acc + lax.optimization_barrier(jnp.sum(kernel_of(rows_block), axis=0)), None)
    col_part, _ = lax.scan(first_sweep, jnp.zeros((K,), jnp.float32), item_blocks)
    numerator = jnp.zeros((K, D), jnp.float32)
    for sweep_index in range(ITERS):
        col_scale = 1.0 / (K * col_part)
        final_turn = sweep_index == ITERS - 1

        def sweep(carry, rows_block):
            col_acc, numer_acc = carry
            kernel_block = kernel_of(rows_block)
            row_part = jnp.dot(kernel_block, col_scale, precision=lax.Precision.HIGHEST, preferred_element_type=jnp.float32)
            row_scale = 1.0 / (ITEMS * row_part)
            col_acc = col_acc + jnp.dot(row_scale, kernel_block, precision=lax.Precision.HIGHEST, preferred_element_type=jnp.float32)
            if final_turn:
                numer_acc = numer_acc + jnp.dot(kernel_block.T, row_scale[:, None] * rows_block, precision=lax.Precision.HIGHEST, preferred_element_type=jnp.float32)
            return ((col_acc, numer_acc), None)
        (col_part, numerator), _ = lax.scan(sweep, (jnp.zeros((K,), jnp.float32), jnp.zeros((K, D), jnp.float32)), item_blocks)
    new_codewords = numerator / col_part[:, None]
    residual = items - jnp.take(codewords, assign.astype(jnp.int32), axis=0)
    return (new_codewords, residual)
```

```python
import functools

import jax
import jax.numpy as jnp
from jax import lax
from jax.experimental import pallas as pl
from jax.experimental.pallas import tpu as pltpu
from jax.sharding import PartitionSpec as P

ITERS = 3
LANES = 128
PARTS = 4
EPSILON = 1e-05
INVERSE_TEMP = 64.0
MESH = pl.DeviceIdType.MESH
F32, BF16 = jnp.float32, jnp.bfloat16


def unit_rows(values):
    return values * lax.rsqrt(jnp.mean(values * values, axis=-1, keepdims=True) + EPSILON)


def split(values):
    high = values.astype(BF16)
    return high, (values - high.astype(F32)).astype(BF16)


def dot(left, right, contract):
    return lax.dot_general(left, right, ((contract[:1], contract[1:]), ((), ())), preferred_element_type=F32)


def kernel(A, B, C, items_ref, code_ref, assign_ref, out_ref, looked_ref,
           cw, chi, clo, xs, xcat, kf, khi, klo, pick, pickr, colb, cola, rowx, rz, massb, xt, wcat,
           num, numc, numx, numr,
           load_sem, y_send, y_recv, z_send, z_recv, f_send, f_recv, p_send, p_recv,
           b_send, b_recv, a_send, a_recv, r_send, r_recv, rz_send, rz_recv, c_send, c_recv, h_send, h_recv):
    R, D = items_ref.shape
    L = code_ref.shape[0]
    G = C * R
    N = A * B
    H = B // 2
    d = D // N
    W = D // A
    TL = min(L, max(LANES, 131072 // G))
    tiles = L // TL
    Lq = L // PARTS
    dp, c = lax.axis_index("dp"), lax.axis_index("code")
    line, place = lax.div(dp, B), lax.rem(dp, B)
    outer, core = lax.div(place, 2), lax.rem(place, 2)

    def on_line(off):
        return {"dp": lax.rem(line + off, A) * B + place}

    def on_place(off):
        return {"dp": line * B + lax.rem(place + off, B)}

    def on_code(off):
        return {"code": lax.rem(c + off, C)}

    def on_outer(off):
        return {"dp": line * B + lax.rem(outer + off, H) * 2 + core}

    def remote(src, dst, send, recv, where):
        return pltpu.make_async_remote_copy(src_ref=src, dst_ref=dst, send_sem=send, recv_sem=recv,
                                            device_id=where, device_id_type=MESH)

    def start(copies):
        for copy in copies:
            copy.start()
        return copies

    def wait(copies):
        for copy in copies:
            copy.wait()

    rows = L // PARTS
    loads = [pltpu.make_async_copy(code_ref.at[pl.ds(q * rows, rows)], cw.at[pl.ds(q * rows, rows)], load_sem.at[q])
             for q in range(PARTS)]
    start(loads)
    barrier = pltpu.get_barrier_semaphore()
    peers = [on_line(o) for o in range(1, A)] + [on_place(o) for o in range(1, B)] + [on_code(o) for o in range(1, C)]
    for peer in peers:
        pl.semaphore_signal(barrier, inc=1, device_id=peer, device_id_type=MESH)
    pl.semaphore_wait(barrier, len(peers))

    y_copies = start([remote(items_ref, xs.at[0, o], y_send.at[o], y_recv.at[o], on_code(o)) for o in range(1, C)])
    z_copies = start([remote(items_ref, xs.at[o, 0], z_send.at[o], z_recv.at[o], on_line(o)) for o in range(1, A)])
    xs[0, 0] = items_ref[...]

    for q in range(PARTS):
        loads[q].wait()

        def scale(j, _):
            at = pl.ds(pl.multiple_of(q * rows + j * LANES, LANES), LANES)
            chi[at, :], clo[at, :] = split(unit_rows(cw[at, :]) * (INVERSE_TEMP / D))
            return 0
        lax.fori_loop(0, rows // LANES, scale, 0)

    def pick_for(off):
        base = lax.rem(c + off, C) * R

        def one(i, _):
            index = assign_ref[base + i] - c * L
            inside = (index >= 0) & (index < L)
            row = cw[pl.ds(jnp.clip(index, 0, L - 1), 1), :]
            pick[off, pl.ds(i, 1), :] = jnp.where(inside, row, 0.0)
            return 0
        lax.fori_loop(0, R, one, 0, unroll=8)

    for o in range(1, C):
        pick_for(o)
    p_copies = start([remote(pick.at[o], pickr.at[o], p_send.at[o], p_recv.at[o], on_code(o)) for o in range(1, C)])
    pick_for(0)

    def prepare(slot):
        for s in range(C):
            high, low = split(unit_rows(xs[slot, s]))
            xcat[s * R:(s + 1) * R, :] = high
            xcat[G + s * R:G + (s + 1) * R, :] = low
            part = xs[slot, s, :, pl.ds(pl.multiple_of(line * W, LANES), W)]
            xt[:, slot * G + s * R:slot * G + (s + 1) * R] = part.T

    def similar(slot, lo, hi, own=False):
        def step(j, _):
            at = pl.ds(pl.multiple_of(j * TL, LANES), TL)
            both = dot(xcat[...], chi[at, :], (1, 1))
            vals = jnp.exp(both[:G] + both[G:] + dot(xcat[:G, :], clo[at, :], (1, 1)))
            high, low = split(vals)
            khi[slot * G:(slot + 1) * G, at] = high
            klo[slot * G:(slot + 1) * G, at] = low
            if own:
                kf[:, at] = vals
                colb[0, 0, :, at] = jnp.sum(vals, axis=0, keepdims=True)
            return 0
        lax.fori_loop(lo, hi, step, 0)

    wait(y_copies)
    prepare(0)
    similar(0, 0, tiles, True)

    def start_b(t):
        return start([remote(colb.at[t, 0], colb.at[t, o], b_send.at[t, o], b_recv.at[t, o], on_place(o))
                      for o in range(1, B)])

    def start_a(t):
        total = colb[t, 0]
        for o in range(1, B):
            total = total + colb[t, o]
        cola[t, 0] = total
        return start([remote(cola.at[t, 0], cola.at[t, o], a_send.at[t, o], a_recv.at[t, o], on_line(o))
                      for o in range(1, A)])

    def column_total(t):
        total = cola[t, 0]
        for o in range(1, A):
            total = total + cola[t, o]
        return total

    forwards = {}

    def forward(o):
        z_copies[o - 1].wait()
        forwards[o] = start([remote(xs.at[o, 0], xs.at[o, s], f_send.at[o, s], f_recv.at[o, s], on_code(s))
                             for s in range(1, C)])

    def begin_block(o, lo, hi):
        if lo == 0:
            wait(forwards[o])
            prepare(o)
        similar(o, lo, hi)

    half = tiles // 2
    work = [[lambda o=o: forward(o)] for o in range(1, A)]
    for o in range(1, A):
        work.append([lambda o=o: begin_block(o, 0, half)])
        work.append([lambda o=o: begin_block(o, half, tiles)])

    def background():
        if work:
            for job in work.pop(0):
                job()

    for t in range(ITERS):
        copies = start_b(t)
        background()
        wait(copies)
        copies = start_a(t)
        background()
        wait(copies)
        massb[...] = 1.0 / (C * L * column_total(t))

        def row_step(j, acc):
            at = pl.ds(pl.multiple_of(j * LANES, LANES), LANES)
            return acc + kf[:, at] * massb[:, at]
        acc = lax.fori_loop(0, L // LANES, row_step, jnp.zeros((G, LANES), F32), unroll=4)
        rowx[t, 0] = jnp.sum(acc.T, axis=0, keepdims=True)
        copies = start([remote(rowx.at[t, 0], rowx.at[t, o], r_send.at[t, o], r_recv.at[t, o], on_code(o))
                        for o in range(1, C)])
        background()
        wait(copies)
        total = rowx[t, 0]
        for o in range(1, C):
            came = rowx[t, o]
            total = total + jnp.concatenate([came[:, G - o * R:], came[:, :G - o * R]], axis=1)
        row_scale = 1.0 / (N * G * total)
        if t == ITERS - 1:
            rz[0] = row_scale
            rz_copies = start([remote(rz.at[0], rz.at[o], rz_send.at[o], rz_recv.at[o], on_line(o))
                               for o in range(1, A)])
        spread = jnp.broadcast_to(row_scale, (LANES, G)).T

        def col_step(j, _):
            at = pl.ds(pl.multiple_of(j * LANES, LANES), LANES)
            colb[t + 1, 0, :, at] = jnp.sum(kf[:, at] * spread, axis=0, keepdims=True)
            return 0
        lax.fori_loop(0, L // LANES, col_step, 0, unroll=4)

    copies = start_b(ITERS)
    while work:
        background()
    wait(rz_copies)
    for o in range(A):
        high, low = split(xt[:, o * G:(o + 1) * G] * rz[o])
        wcat[:W, o * G:(o + 1) * G] = high
        wcat[W:, o * G:(o + 1) * G] = low

    def weighted(q):
        def step(j, _):
            TN = min(Lq, 512)
            src = pl.ds(pl.multiple_of(q * Lq + j * TN, LANES), TN)
            dst = pl.ds(pl.multiple_of(j * TN, LANES), TN)
            both = dot(wcat[...], khi[:, src], (1, 0))
            vals = both[:W] + both[W:] + dot(wcat[:W, :], klo[:, src], (1, 0))
            for g in range(B):
                num[q, g % 2, g // 2, :, dst] = vals[g * d:(g + 1) * d]
            return 0
        lax.fori_loop(0, Lq // min(Lq, 512), step, 0)
        return start([remote(num.at[q, 1 - core], numc.at[q], c_send.at[q], c_recv.at[q],
                             {"dp": line * B + outer * 2 + (1 - core)})])

    def exchange(q):
        numx[q] = num[q, core] + numc[q]
        return start([remote(numx.at[q, lax.rem(outer + o, H)], numr.at[q, o], h_send.at[q, o], h_recv.at[q, o],
                             on_outer(o)) for o in range(1, H)])

    core_copies, outer_copies = [], []
    for q in range(PARTS):
        core_copies.append(weighted(q))
        if q == 0:
            wait(copies)
            copies = start_a(ITERS)
        else:
            wait(core_copies[q - 1])
            outer_copies.append(exchange(q - 1))
    wait(core_copies[PARTS - 1])
    outer_copies.append(exchange(PARTS - 1))
    wait(p_copies)
    looked = pick[0]
    for o in range(1, C):
        looked = looked + pickr[o]
    looked_ref[...] = looked
    wait(copies)
    massb[...] = 1.0 / column_total(ITERS)
    for q in range(PARTS):
        wait(outer_copies[q])
        total = numx[q, outer]
        for o in range(1, H):
            total = total + numr[q, o]
        out_ref[:, q * Lq:(q + 1) * Lq] = total * massb[:, q * Lq:(q + 1) * Lq]


def body(items, codewords, assign):
    C, N = lax.axis_size("code"), lax.axis_size("dp")
    R, D = items.shape
    L = codewords.shape[0]
    A = D // LANES
    B, G, d, H, Lq = N // A, C * R, D // N, N // A // 2, L // PARTS
    dma = pltpu.SemaphoreType.DMA
    T = ITERS + 1
    flops = 2 * 3 * A * G * L * (D + LANES)
    out, looked = pl.pallas_call(
        functools.partial(kernel, A, B, C),
        out_shape=(jax.ShapeDtypeStruct((d, L), F32), jax.ShapeDtypeStruct((R, D), F32)),
        in_specs=[pl.BlockSpec(memory_space=pltpu.VMEM), pl.BlockSpec(memory_space=pl.ANY),
                  pl.BlockSpec(memory_space=pltpu.SMEM)],
        out_specs=[pl.BlockSpec(memory_space=pltpu.VMEM)] * 2,
        scratch_shapes=[
            pltpu.VMEM((L, D), F32), pltpu.VMEM((L, D), BF16), pltpu.VMEM((L, D), BF16),
            pltpu.VMEM((A, C, R, D), F32), pltpu.VMEM((2 * G, D), BF16),
            pltpu.VMEM((G, L), F32), pltpu.VMEM((A * G, L), BF16), pltpu.VMEM((A * G, L), BF16),
            pltpu.VMEM((C, R, D), F32), pltpu.VMEM((C, R, D), F32),
            pltpu.VMEM((T, B, 1, L), F32), pltpu.VMEM((T, A, 1, L), F32),
            pltpu.VMEM((ITERS, C, 1, G), F32), pltpu.VMEM((A, 1, G), F32), pltpu.VMEM((1, L), F32),
            pltpu.VMEM((D // A, A * G), F32), pltpu.VMEM((2 * (D // A), A * G), BF16),
            pltpu.VMEM((PARTS, 2, H, d, Lq), F32), pltpu.VMEM((PARTS, H, d, Lq), F32),
            pltpu.VMEM((PARTS, H, d, Lq), F32), pltpu.VMEM((PARTS, H, d, Lq), F32),
            dma((PARTS,)), dma((C,)), dma((C,)), dma((A,)), dma((A,)), dma((A, C)), dma((A, C)), dma((C,)), dma((C,)),
            dma((T, B)), dma((T, B)), dma((T, A)), dma((T, A)), dma((ITERS, C)), dma((ITERS, C)),
            dma((A,)), dma((A,)), dma((PARTS,)), dma((PARTS,)), dma((PARTS, H)), dma((PARTS, H)),
        ],
        compiler_params=pltpu.CompilerParams(collective_id=0, has_side_effects=True,
                                             vmem_limit_bytes=60 * 1024 * 1024),
        cost_estimate=pl.CostEstimate(flops=flops, bytes_accessed=4 * (L * D + 4 * R * D), transcendentals=A * G * L),
        name="sinkhorn_level",
    )(items, codewords, assign)
    return out.T, items - looked


def solution(mesh):
    in_specs = (P(("dp", "code"), None), P("code", None), P("dp"))
    out_specs = (P("code", "dp"), P(("dp", "code"), None))
    return jax.shard_map(body, mesh=mesh, in_specs=in_specs, out_specs=out_specs, check_vma=False)
```

```python
import functools

import jax
import jax.numpy as jnp
from jax import lax
from jax.experimental import pallas as pl
from jax.experimental.pallas import tpu as pltpu
from jax.sharding import PartitionSpec as P

ITERS = 3
LANES = 128
PARTS = 4
EPSILON = 1e-05
INVERSE_TEMP = 64.0
MESH = pl.DeviceIdType.MESH
F32, BF16 = jnp.float32, jnp.bfloat16


def unit_rows(values):
    return values * lax.rsqrt(jnp.mean(values * values, axis=-1, keepdims=True) + EPSILON)


def split(values):
    high = values.astype(BF16)
    return high, (values - high.astype(F32)).astype(BF16)


def dot(left, right, contract):
    return lax.dot_general(left, right, ((contract[:1], contract[1:]), ((), ())), preferred_element_type=F32)


def kernel(A, B, C, items_ref, code_ref, assign_ref, out_ref, looked_ref,
           cw, chi, clo, xs, xcat, kf, khi, klo, pick, pickr, colb, cola, rowx, rz, massb, xt, wcat,
           num, numc, numx, numr,
           load_sem, y_send, y_recv, z_send, z_recv, f_send, f_recv, p_send, p_recv,
           b_send, b_recv, a_send, a_recv, r_send, r_recv, rz_send, rz_recv, c_send, c_recv, h_send, h_recv):
    R, D = items_ref.shape
    L = code_ref.shape[0]
    G = C * R
    N = A * B
    H = B // 2
    d = D // N
    W = D // A
    TL = min(L, max(LANES, 131072 // G))
    tiles = L // TL
    Lq = L // PARTS
    dp, c = lax.axis_index("dp"), lax.axis_index("code")
    line, place = lax.div(dp, B), lax.rem(dp, B)
    outer, core = lax.div(place, 2), lax.rem(place, 2)

    def on_line(off):
        return {"dp": lax.rem(line + off, A) * B + place}

    def on_place(off):
        return {"dp": line * B + lax.rem(place + off, B)}

    def on_code(off):
        return {"code": lax.rem(c + off, C)}

    def on_outer(off):
        return {"dp": line * B + lax.rem(outer + off, H) * 2 + core}

    def remote(src, dst, send, recv, where):
        return pltpu.make_async_remote_copy(src_ref=src, dst_ref=dst, send_sem=send, recv_sem=recv,
                                            device_id=where, device_id_type=MESH)

    def start(copies):
        for copy in copies:
            copy.start()
        return copies

    def wait(copies):
        for copy in copies:
            copy.wait()

    rows = L // PARTS
    loads = [pltpu.make_async_copy(code_ref.at[pl.ds(q * rows, rows)], cw.at[pl.ds(q * rows, rows)], load_sem.at[q])
             for q in range(PARTS)]
    start(loads)
    barrier = pltpu.get_barrier_semaphore()
    peers = [on_line(o) for o in range(1, A)] + [on_place(o) for o in range(1, B)] + [on_code(o) for o in range(1, C)]
    for peer in peers:
        pl.semaphore_signal(barrier, inc=1, device_id=peer, device_id_type=MESH)
    pl.semaphore_wait(barrier, len(peers))

    y_copies = start([remote(items_ref, xs.at[0, o], y_send.at[o], y_recv.at[o], on_code(o)) for o in range(1, C)])
    near = sorted(range(1, A), key=lambda o: min(o, A - o))
    z_copies = {o: remote(items_ref, xs.at[o, 0], z_send.at[o], z_recv.at[o], on_line(o)) for o in near}
    start([z_copies[o] for o in near[:2]])
    xs[0, 0] = items_ref[...]

    for q in range(PARTS):
        loads[q].wait()

        def scale(j, _):
            at = pl.ds(pl.multiple_of(q * rows + j * LANES, LANES), LANES)
            chi[at, :], clo[at, :] = split(unit_rows(cw[at, :]) * (INVERSE_TEMP / D))
            return 0
        lax.fori_loop(0, rows // LANES, scale, 0)

    def pick_for(off):
        base = lax.rem(c + off, C) * R

        def one(i, _):
            index = assign_ref[base + i] - c * L
            inside = (index >= 0) & (index < L)
            row = cw[pl.ds(jnp.clip(index, 0, L - 1), 1), :]
            pick[off, pl.ds(i, 1), :] = jnp.where(inside, row, 0.0)
            return 0
        lax.fori_loop(0, R, one, 0, unroll=8)

    p_copies = [remote(pick.at[o], pickr.at[o], p_send.at[o], p_recv.at[o], on_code(o)) for o in range(1, C)]

    def prepare(slot):
        for s in range(C):
            high, low = split(unit_rows(xs[slot, s]))
            xcat[s * R:(s + 1) * R, :] = high
            xcat[G + s * R:G + (s + 1) * R, :] = low
            part = xs[slot, s, :, pl.ds(pl.multiple_of(line * W, LANES), W)]
            xt[:, slot * G + s * R:slot * G + (s + 1) * R] = part.T

    def similar(slot, lo, hi, own=False):
        def step(j, _):
            at = pl.ds(pl.multiple_of(j * TL, LANES), TL)
            both = dot(xcat[...], chi[at, :], (1, 1))
            vals = jnp.exp(both[:G] + both[G:] + dot(xcat[:G, :], clo[at, :], (1, 1)))
            high, low = split(vals)
            khi[slot * G:(slot + 1) * G, at] = high
            klo[slot * G:(slot + 1) * G, at] = low
            if own:
                kf[:, at] = vals
                colb[0, 0, :, at] = jnp.sum(vals, axis=0, keepdims=True)
            return 0
        lax.fori_loop(lo, hi, step, 0)

    wait(y_copies)
    prepare(0)
    similar(0, 0, tiles, True)

    def start_b(t):
        return start([remote(colb.at[t, 0], colb.at[t, o], b_send.at[t, o], b_recv.at[t, o], on_place(o))
                      for o in range(1, B)])

    def start_a(t):
        total = colb[t, 0]
        for o in range(1, B):
            total = total + colb[t, o]
        cola[t, 0] = total
        return start([remote(cola.at[t, 0], cola.at[t, o], a_send.at[t, o], a_recv.at[t, o], on_line(o))
                      for o in range(1, A)])

    def column_total(t):
        total = cola[t, 0]
        for o in range(1, A):
            total = total + cola[t, o]
        return total

    forwards = {}

    def forward(o):
        z_copies[o].wait()
        forwards[o] = start([remote(xs.at[o, 0], xs.at[o, s], f_send.at[o, s], f_recv.at[o, s], on_code(s))
                             for s in range(1, C)])

    def begin_block(o, lo, hi):
        if lo == 0:
            wait(forwards[o])
            prepare(o)
        similar(o, lo, hi)

    half = tiles // 2
    def pick_all():
        for o in range(C):
            pick_for(o)

    work = [[lambda: forward(near[0]), lambda: start([z_copies[o] for o in near[2:]])], [pick_all],
            [lambda: forward(near[1])]]
    for o in near:
        work.append([lambda o=o: begin_block(o, 0, half)])
        work.append([lambda o=o: begin_block(o, half, tiles)])
    work[3] = [lambda o=o: forward(o) for o in near[2:]] + [lambda: start(p_copies)] + work[3]

    def background():
        if work:
            for job in work.pop(0):
                job()

    for t in range(ITERS):
        copies = start_b(t)
        background()
        wait(copies)
        copies = start_a(t)
        background()
        wait(copies)
        massb[...] = 1.0 / (C * L * column_total(t))

        def row_step(j, acc):
            at = pl.ds(pl.multiple_of(j * LANES, LANES), LANES)
            return acc + kf[:, at] * massb[:, at]
        acc = lax.fori_loop(0, L // LANES, row_step, jnp.zeros((G, LANES), F32), unroll=4)
        rowx[t, 0] = jnp.sum(acc.T, axis=0, keepdims=True)
        copies = start([remote(rowx.at[t, 0], rowx.at[t, o], r_send.at[t, o], r_recv.at[t, o], on_code(o))
                        for o in range(1, C)])
        background()
        wait(copies)
        total = rowx[t, 0]
        for o in range(1, C):
            came = rowx[t, o]
            total = total + jnp.concatenate([came[:, G - o * R:], came[:, :G - o * R]], axis=1)
        row_scale = 1.0 / (N * G * total)
        if t == ITERS - 1:
            rz[0] = row_scale
            rz_copies = start([remote(rz.at[0], rz.at[o], rz_send.at[o], rz_recv.at[o], on_line(o))
                               for o in range(1, A)])
        spread = jnp.broadcast_to(row_scale, (LANES, G)).T

        def col_step(j, _):
            at = pl.ds(pl.multiple_of(j * LANES, LANES), LANES)
            colb[t + 1, 0, :, at] = jnp.sum(kf[:, at] * spread, axis=0, keepdims=True)
            return 0
        lax.fori_loop(0, L // LANES, col_step, 0, unroll=4)

    copies = start_b(ITERS)
    while work:
        background()
    wait(rz_copies)
    for o in range(A):
        high, low = split(xt[:, o * G:(o + 1) * G] * rz[o])
        wcat[:W, o * G:(o + 1) * G] = high
        wcat[W:, o * G:(o + 1) * G] = low

    def weighted(q):
        def step(j, _):
            TN = min(Lq, 512)
            src = pl.ds(pl.multiple_of(q * Lq + j * TN, LANES), TN)
            dst = pl.ds(pl.multiple_of(j * TN, LANES), TN)
            both = dot(wcat[...], khi[:, src], (1, 0))
            vals = both[:W] + both[W:] + dot(wcat[:W, :], klo[:, src], (1, 0))
            for g in range(B):
                num[q, g % 2, g // 2, :, dst] = vals[g * d:(g + 1) * d]
            return 0
        lax.fori_loop(0, Lq // min(Lq, 512), step, 0)
        return start([remote(num.at[q, 1 - core], numc.at[q], c_send.at[q], c_recv.at[q],
                             {"dp": line * B + outer * 2 + (1 - core)})])

    def exchange(q):
        numx[q] = num[q, core] + numc[q]
        return start([remote(numx.at[q, lax.rem(outer + o, H)], numr.at[q, o], h_send.at[q, o], h_recv.at[q, o],
                             on_outer(o)) for o in range(1, H)])

    core_copies, outer_copies = [], []
    for q in range(PARTS):
        core_copies.append(weighted(q))
        if q == 0:
            wait(copies)
            copies = start_a(ITERS)
        else:
            wait(core_copies[q - 1])
            outer_copies.append(exchange(q - 1))
    wait(core_copies[PARTS - 1])
    outer_copies.append(exchange(PARTS - 1))
    wait(p_copies)
    looked = pick[0]
    for o in range(1, C):
        looked = looked + pickr[o]
    looked_ref[...] = looked
    wait(copies)
    massb[...] = 1.0 / column_total(ITERS)
    for q in range(PARTS):
        wait(outer_copies[q])
        total = numx[q, outer]
        for o in range(1, H):
            total = total + numr[q, o]
        out_ref[:, q * Lq:(q + 1) * Lq] = total * massb[:, q * Lq:(q + 1) * Lq]


def finish(total_ref, items_ref, looked_ref, out_ref, residual_ref):
    out_ref[...] = total_ref[...]
    residual_ref[...] = items_ref[...] - looked_ref[...]


def body(items, codewords, assign):
    C, N = lax.axis_size("code"), lax.axis_size("dp")
    R, D = items.shape
    L = codewords.shape[0]
    A = D // LANES
    B, G, d, H, Lq = N // A, C * R, D // N, N // A // 2, L // PARTS
    dma = pltpu.SemaphoreType.DMA
    T = ITERS + 1
    flops = 2 * 3 * A * G * L * (D + LANES)
    out, looked = pl.pallas_call(
        functools.partial(kernel, A, B, C),
        out_shape=(jax.ShapeDtypeStruct((d, L), F32), jax.ShapeDtypeStruct((R, D), F32)),
        in_specs=[pl.BlockSpec(memory_space=pltpu.VMEM), pl.BlockSpec(memory_space=pl.ANY),
                  pl.BlockSpec(memory_space=pltpu.SMEM)],
        out_specs=[pl.BlockSpec(memory_space=pltpu.VMEM)] * 2,
        scratch_shapes=[
            pltpu.VMEM((L, D), F32), pltpu.VMEM((L, D), BF16), pltpu.VMEM((L, D), BF16),
            pltpu.VMEM((A, C, R, D), F32), pltpu.VMEM((2 * G, D), BF16),
            pltpu.VMEM((G, L), F32), pltpu.VMEM((A * G, L), BF16), pltpu.VMEM((A * G, L), BF16),
            pltpu.VMEM((C, R, D), F32), pltpu.VMEM((C, R, D), F32),
            pltpu.VMEM((T, B, 1, L), F32), pltpu.VMEM((T, A, 1, L), F32),
            pltpu.VMEM((ITERS, C, 1, G), F32), pltpu.VMEM((A, 1, G), F32), pltpu.VMEM((1, L), F32),
            pltpu.VMEM((D // A, A * G), F32), pltpu.VMEM((2 * (D // A), A * G), BF16),
            pltpu.VMEM((PARTS, 2, H, d, Lq), F32), pltpu.VMEM((PARTS, H, d, Lq), F32),
            pltpu.VMEM((PARTS, H, d, Lq), F32), pltpu.VMEM((PARTS, H, d, Lq), F32),
            dma((PARTS,)), dma((C,)), dma((C,)), dma((A,)), dma((A,)), dma((A, C)), dma((A, C)), dma((C,)), dma((C,)),
            dma((T, B)), dma((T, B)), dma((T, A)), dma((T, A)), dma((ITERS, C)), dma((ITERS, C)),
            dma((A,)), dma((A,)), dma((PARTS,)), dma((PARTS,)), dma((PARTS, H)), dma((PARTS, H)),
        ],
        compiler_params=pltpu.CompilerParams(collective_id=0, has_side_effects=True,
                                             vmem_limit_bytes=60 * 1024 * 1024),
        cost_estimate=pl.CostEstimate(flops=flops, bytes_accessed=4 * (L * D + 4 * R * D), transcendentals=A * G * L),
        name="sinkhorn_level",
    )(items, codewords, assign)
    new_codewords, residual = pl.pallas_call(
        finish,
        out_shape=(jax.ShapeDtypeStruct((d, L), F32), jax.ShapeDtypeStruct((R, D), F32)),
        in_specs=[pl.BlockSpec(memory_space=pltpu.VMEM)] * 3,
        out_specs=[pl.BlockSpec(memory_space=pltpu.VMEM)] * 2,
        name="write_outputs",
    )(out, items, looked)
    return new_codewords.T, residual


def solution(mesh):
    in_specs = (P(("dp", "code"), None), P("code", None), P("dp"))
    out_specs = (P("code", "dp"), P(("dp", "code"), None))
    return jax.shard_map(body, mesh=mesh, in_specs=in_specs, out_specs=out_specs, check_vma=False)
```

```python
import functools

import jax
import jax.numpy as jnp
from jax import lax
from jax.experimental import pallas as pl
from jax.experimental.pallas import tpu as pltpu
from jax.sharding import PartitionSpec as P

ITERS = 3
LANES = 128
PARTS = 4
EPSILON = 1e-05
INVERSE_TEMP = 64.0
MESH = pl.DeviceIdType.MESH
F32, BF16 = jnp.float32, jnp.bfloat16


def unit_rows(values):
    return values * lax.rsqrt(jnp.mean(values * values, axis=-1, keepdims=True) + EPSILON)


def split(values):
    high = values.astype(BF16)
    return high, (values - high.astype(F32)).astype(BF16)


def dot(left, right, contract):
    return lax.dot_general(left, right, ((contract[:1], contract[1:]), ((), ())), preferred_element_type=F32)


def kernel(A, B, C, items_ref, code_ref, assign_ref, out_ref, looked_ref,
           cw, ccat, xs, xcat, kf, khi, klo, pick, pickr, colb, cola, rowx, rz, massb, xt, wcat,
           num, numc, numx, numr,
           load_sem, y_send, y_recv, z_send, z_recv, f_send, f_recv, p_send, p_recv,
           b_send, b_recv, a_send, a_recv, r_send, r_recv, rz_send, rz_recv, c_send, c_recv, h_send, h_recv):
    R, D = items_ref.shape
    L = code_ref.shape[0]
    G = C * R
    N = A * B
    H = B // 2
    d = D // N
    W = D // A
    TL = min(L, max(LANES, 65536 // G))
    tiles = L // TL
    Lq = L // PARTS
    dp, c = lax.axis_index("dp"), lax.axis_index("code")
    line, place = lax.div(dp, B), lax.rem(dp, B)
    outer, core = lax.div(place, 2), lax.rem(place, 2)

    def on_line(off):
        return {"dp": lax.rem(line + off, A) * B + place}

    def on_place(off):
        return {"dp": line * B + lax.rem(place + off, B)}

    def on_code(off):
        return {"code": lax.rem(c + off, C)}

    def on_outer(off):
        return {"dp": line * B + lax.rem(outer + off, H) * 2 + core}

    def remote(src, dst, send, recv, where):
        return pltpu.make_async_remote_copy(src_ref=src, dst_ref=dst, send_sem=send, recv_sem=recv,
                                            device_id=where, device_id_type=MESH)

    def start(copies):
        for copy in copies:
            copy.start()
        return copies

    def wait(copies):
        for copy in copies:
            copy.wait()

    rows = L // PARTS
    loads = [pltpu.make_async_copy(code_ref.at[pl.ds(q * rows, rows)], cw.at[pl.ds(q * rows, rows)], load_sem.at[q])
             for q in range(PARTS)]
    start(loads)
    barrier = pltpu.get_barrier_semaphore()
    peers = [on_line(o) for o in range(1, A)] + [on_place(o) for o in range(1, B)] + [on_code(o) for o in range(1, C)]
    for peer in peers:
        pl.semaphore_signal(barrier, inc=1, device_id=peer, device_id_type=MESH)
    pl.semaphore_wait(barrier, len(peers))

    y_copies = start([remote(items_ref, xs.at[0, o], y_send.at[o], y_recv.at[o], on_code(o)) for o in range(1, C)])
    near = sorted(range(1, A), key=lambda o: min(o, A - o))
    z_copies = {o: remote(items_ref, xs.at[o, 0], z_send.at[o], z_recv.at[o], on_line(o)) for o in near}
    start([z_copies[o] for o in near[:2]])
    xs[0, 0] = items_ref[...]

    for q in range(PARTS):
        loads[q].wait()

        def scale(j, _):
            at = pl.ds(pl.multiple_of(q * rows + j * LANES, LANES), LANES)
            high, low = split(unit_rows(cw[at, :]) * (INVERSE_TEMP / D))
            ccat[at, :D] = high
            ccat[at, D:2 * D] = high
            ccat[at, 2 * D:] = low
            return 0
        lax.fori_loop(0, rows // LANES, scale, 0)

    def pick_for(off):
        base = lax.rem(c + off, C) * R

        def one(i, _):
            index = assign_ref[base + i] - c * L
            inside = (index >= 0) & (index < L)
            row = cw[pl.ds(jnp.clip(index, 0, L - 1), 1), :]
            pick[off, pl.ds(i, 1), :] = jnp.where(inside, row, 0.0)
            return 0
        lax.fori_loop(0, R, one, 0, unroll=8)

    p_copies = [remote(pick.at[o], pickr.at[o], p_send.at[o], p_recv.at[o], on_code(o)) for o in range(1, C)]

    def prepare(slot):
        for s in range(C):
            high, low = split(unit_rows(xs[slot, s]))
            xcat[s * R:(s + 1) * R, :D] = high
            xcat[s * R:(s + 1) * R, D:2 * D] = low
            xcat[s * R:(s + 1) * R, 2 * D:] = high
            part = xs[slot, s, :, pl.ds(pl.multiple_of(line * W, LANES), W)]
            xt[:, slot * G + s * R:slot * G + (s + 1) * R] = part.T

    def similar(slot, lo, hi, own=False):
        def step(j, _):
            at = pl.ds(pl.multiple_of(j * TL, LANES), TL)
            vals = jnp.exp(dot(xcat[...], ccat[at, :], (1, 1)))
            high, low = split(vals)
            khi[slot * G:(slot + 1) * G, at] = high
            klo[slot * G:(slot + 1) * G, at] = low
            if own:
                kf[:, at] = vals
                colb[0, 0, :, at] = jnp.sum(vals, axis=0, keepdims=True)
            return 0
        lax.fori_loop(lo, hi, step, 0, unroll=4)

    wait(y_copies)
    prepare(0)
    similar(0, 0, tiles, True)

    def start_b(t):
        return start([remote(colb.at[t, 0], colb.at[t, o], b_send.at[t, o], b_recv.at[t, o], on_place(o))
                      for o in range(1, B)])

    def start_a(t):
        total = colb[t, 0]
        for o in range(1, B):
            total = total + colb[t, o]
        cola[t, 0] = total
        return start([remote(cola.at[t, 0], cola.at[t, o], a_send.at[t, o], a_recv.at[t, o], on_line(o))
                      for o in range(1, A)])

    def column_total(t):
        total = cola[t, 0]
        for o in range(1, A):
            total = total + cola[t, o]
        return total

    forwards = {}

    def forward(o):
        z_copies[o].wait()
        forwards[o] = start([remote(xs.at[o, 0], xs.at[o, s], f_send.at[o, s], f_recv.at[o, s], on_code(s))
                             for s in range(1, C)])

    def begin_block(o, lo, hi):
        if lo == 0:
            wait(forwards[o])
            prepare(o)
        similar(o, lo, hi)

    half = tiles // 2
    def pick_all():
        for o in range(C):
            pick_for(o)

    work = [[lambda: forward(near[0]), lambda: start([z_copies[o] for o in near[2:]])], [pick_all],
            [lambda: forward(near[1])]]
    for o in near:
        work.append([lambda o=o: begin_block(o, 0, half)])
        work.append([lambda o=o: begin_block(o, half, tiles)])
    work[3] = [lambda o=o: forward(o) for o in near[2:]] + [lambda: start(p_copies)] + work[3]

    def background():
        if work:
            for job in work.pop(0):
                job()

    for t in range(ITERS):
        copies = start_b(t)
        background()
        wait(copies)
        copies = start_a(t)
        background()
        wait(copies)
        massb[...] = 1.0 / (C * L * column_total(t))

        def row_step(j, acc):
            at = pl.ds(pl.multiple_of(j * LANES, LANES), LANES)
            return acc + kf[:, at] * massb[:, at]
        acc = lax.fori_loop(0, L // LANES, row_step, jnp.zeros((G, LANES), F32), unroll=4)
        rowx[t, 0] = jnp.sum(acc.T, axis=0, keepdims=True)
        copies = start([remote(rowx.at[t, 0], rowx.at[t, o], r_send.at[t, o], r_recv.at[t, o], on_code(o))
                        for o in range(1, C)])
        background()
        wait(copies)
        total = rowx[t, 0]
        for o in range(1, C):
            came = rowx[t, o]
            total = total + jnp.concatenate([came[:, G - o * R:], came[:, :G - o * R]], axis=1)
        row_scale = 1.0 / (N * G * total)
        if t == ITERS - 1:
            rz[0] = row_scale
            rz_copies = start([remote(rz.at[0], rz.at[o], rz_send.at[o], rz_recv.at[o], on_line(o))
                               for o in range(1, A)])
        spread = jnp.broadcast_to(row_scale, (LANES, G)).T

        def col_step(j, _):
            at = pl.ds(pl.multiple_of(j * LANES, LANES), LANES)
            colb[t + 1, 0, :, at] = jnp.sum(kf[:, at] * spread, axis=0, keepdims=True)
            return 0
        lax.fori_loop(0, L // LANES, col_step, 0, unroll=4)

    copies = start_b(ITERS)
    while work:
        background()
    wait(rz_copies)
    for o in range(A):
        high, low = split(xt[:, o * G:(o + 1) * G] * rz[o])
        wcat[:W, o * G:(o + 1) * G] = high
        wcat[W:, o * G:(o + 1) * G] = low

    def weighted(q):
        def step(j, _):
            TN = min(Lq, 512)
            src = pl.ds(pl.multiple_of(q * Lq + j * TN, LANES), TN)
            dst = pl.ds(pl.multiple_of(j * TN, LANES), TN)
            both = dot(wcat[...], khi[:, src], (1, 0))
            vals = both[:W] + both[W:] + dot(wcat[:W, :], klo[:, src], (1, 0))
            for g in range(B):
                num[q, g % 2, g // 2, :, dst] = vals[g * d:(g + 1) * d]
            return 0
        lax.fori_loop(0, Lq // min(Lq, 512), step, 0)
        return start([remote(num.at[q, 1 - core], numc.at[q], c_send.at[q], c_recv.at[q],
                             {"dp": line * B + outer * 2 + (1 - core)})])

    def exchange(q):
        numx[q] = num[q, core] + numc[q]
        return start([remote(numx.at[q, lax.rem(outer + o, H)], numr.at[q, o], h_send.at[q, o], h_recv.at[q, o],
                             on_outer(o)) for o in range(1, H)])

    core_copies, outer_copies = [], []
    for q in range(PARTS):
        core_copies.append(weighted(q))
        if q == 0:
            wait(copies)
            copies = start_a(ITERS)
        else:
            wait(core_copies[q - 1])
            outer_copies.append(exchange(q - 1))
    wait(core_copies[PARTS - 1])
    outer_copies.append(exchange(PARTS - 1))
    wait(p_copies)
    looked = pick[0]
    for o in range(1, C):
        looked = looked + pickr[o]
    looked_ref[...] = looked
    wait(copies)
    massb[...] = 1.0 / column_total(ITERS)
    for q in range(PARTS):
        wait(outer_copies[q])
        total = numx[q, outer]
        for o in range(1, H):
            total = total + numr[q, o]
        out_ref[:, q * Lq:(q + 1) * Lq] = total * massb[:, q * Lq:(q + 1) * Lq]


def finish(total_ref, items_ref, looked_ref, out_ref, residual_ref):
    out_ref[...] = total_ref[...]
    residual_ref[...] = items_ref[...] - looked_ref[...]


def body(items, codewords, assign):
    C, N = lax.axis_size("code"), lax.axis_size("dp")
    R, D = items.shape
    L = codewords.shape[0]
    A = D // LANES
    B, G, d, H, Lq = N // A, C * R, D // N, N // A // 2, L // PARTS
    dma = pltpu.SemaphoreType.DMA
    T = ITERS + 1
    flops = 2 * 3 * A * G * L * (D + LANES)
    out, looked = pl.pallas_call(
        functools.partial(kernel, A, B, C),
        out_shape=(jax.ShapeDtypeStruct((d, L), F32), jax.ShapeDtypeStruct((R, D), F32)),
        in_specs=[pl.BlockSpec(memory_space=pltpu.VMEM), pl.BlockSpec(memory_space=pl.ANY),
                  pl.BlockSpec(memory_space=pltpu.SMEM)],
        out_specs=[pl.BlockSpec(memory_space=pltpu.VMEM)] * 2,
        scratch_shapes=[
            pltpu.VMEM((L, D), F32), pltpu.VMEM((L, 3 * D), BF16),
            pltpu.VMEM((A, C, R, D), F32), pltpu.VMEM((G, 3 * D), BF16),
            pltpu.VMEM((G, L), F32), pltpu.VMEM((A * G, L), BF16), pltpu.VMEM((A * G, L), BF16),
            pltpu.VMEM((C, R, D), F32), pltpu.VMEM((C, R, D), F32),
            pltpu.VMEM((T, B, 1, L), F32), pltpu.VMEM((T, A, 1, L), F32),
            pltpu.VMEM((ITERS, C, 1, G), F32), pltpu.VMEM((A, 1, G), F32), pltpu.VMEM((1, L), F32),
            pltpu.VMEM((D // A, A * G), F32), pltpu.VMEM((2 * (D // A), A * G), BF16),
            pltpu.VMEM((PARTS, 2, H, d, Lq), F32), pltpu.VMEM((PARTS, H, d, Lq), F32),
            pltpu.VMEM((PARTS, H, d, Lq), F32), pltpu.VMEM((PARTS, H, d, Lq), F32),
            dma((PARTS,)), dma((C,)), dma((C,)), dma((A,)), dma((A,)), dma((A, C)), dma((A, C)), dma((C,)), dma((C,)),
            dma((T, B)), dma((T, B)), dma((T, A)), dma((T, A)), dma((ITERS, C)), dma((ITERS, C)),
            dma((A,)), dma((A,)), dma((PARTS,)), dma((PARTS,)), dma((PARTS, H)), dma((PARTS, H)),
        ],
        compiler_params=pltpu.CompilerParams(collective_id=0, has_side_effects=True,
                                             vmem_limit_bytes=60 * 1024 * 1024),
        cost_estimate=pl.CostEstimate(flops=flops, bytes_accessed=4 * (L * D + 4 * R * D), transcendentals=A * G * L),
        name="sinkhorn_level",
    )(items, codewords, assign)
    new_codewords, residual = pl.pallas_call(
        finish,
        out_shape=(jax.ShapeDtypeStruct((d, L), F32), jax.ShapeDtypeStruct((R, D), F32)),
        in_specs=[pl.BlockSpec(memory_space=pltpu.VMEM)] * 3,
        out_specs=[pl.BlockSpec(memory_space=pltpu.VMEM)] * 2,
        name="write_outputs",
    )(out, items, looked)
    return new_codewords.T, residual


def solution(mesh):
    in_specs = (P(("dp", "code"), None), P("code", None), P("dp"))
    out_specs = (P("code", "dp"), P(("dp", "code"), None))
    return jax.shard_map(body, mesh=mesh, in_specs=in_specs, out_specs=out_specs, check_vma=False)
```

```python
import functools

import jax
import jax.numpy as jnp
from jax import lax
from jax.experimental import pallas as pl
from jax.experimental.pallas import tpu as pltpu
from jax.sharding import PartitionSpec as P

ITERS = 3
LANES = 128
PARTS = 4
EPSILON = 1e-05
INVERSE_TEMP = 64.0
MESH = pl.DeviceIdType.MESH
F32, BF16 = jnp.float32, jnp.bfloat16


def unit_rows(values):
    return values * lax.rsqrt(jnp.mean(values * values, axis=-1, keepdims=True) + EPSILON)


def split(values):
    high = values.astype(BF16)
    return high, (values - high.astype(F32)).astype(BF16)


def dot(left, right, contract):
    return lax.dot_general(left, right, ((contract[:1], contract[1:]), ((), ())), preferred_element_type=F32)


def kernel(A, B, C, items_ref, code_ref, assign_ref, out_ref, looked_ref,
           cw, ccat, xs, xcat, kf, khi, klo, pick, pickr, colb, cola, rowx, rz, massb, xt, wcat,
           num, numc, numx, numr,
           load_sem, y_send, y_recv, z_send, z_recv, f_send, f_recv, p_send, p_recv,
           b_send, b_recv, a_send, a_recv, r_send, r_recv, rz_send, rz_recv, c_send, c_recv, h_send, h_recv):
    R, D = items_ref.shape
    L = code_ref.shape[0]
    G = C * R
    N = A * B
    H = B // 2
    d = D // N
    W = D // A
    TL = min(L, max(LANES, 65536 // G))
    tiles = L // TL
    Lq = L // PARTS
    dp, c = lax.axis_index("dp"), lax.axis_index("code")
    line, place = lax.div(dp, B), lax.rem(dp, B)
    outer, core = lax.div(place, 2), lax.rem(place, 2)

    def on_line(off):
        return {"dp": lax.rem(line + off, A) * B + place}

    def on_place(off):
        return {"dp": line * B + lax.rem(place + off, B)}

    def on_code(off):
        return {"code": lax.rem(c + off, C)}

    def on_outer(off):
        return {"dp": line * B + lax.rem(outer + off, H) * 2 + core}

    def remote(src, dst, send, recv, where):
        return pltpu.make_async_remote_copy(src_ref=src, dst_ref=dst, send_sem=send, recv_sem=recv,
                                            device_id=where, device_id_type=MESH)

    def start(copies):
        for copy in copies:
            copy.start()
        return copies

    def wait(copies):
        for copy in copies:
            copy.wait()

    rows = L // PARTS
    loads = [pltpu.make_async_copy(code_ref.at[pl.ds(q * rows, rows)], cw.at[pl.ds(q * rows, rows)], load_sem.at[q])
             for q in range(PARTS)]
    start(loads)
    barrier = pltpu.get_barrier_semaphore()
    peers = [on_line(o) for o in range(1, A)] + [on_place(o) for o in range(1, B)] + [on_code(o) for o in range(1, C)]
    for peer in peers:
        pl.semaphore_signal(barrier, inc=1, device_id=peer, device_id_type=MESH)
    pl.semaphore_wait(barrier, len(peers))

    y_copies = start([remote(items_ref, xs.at[0, o], y_send.at[o], y_recv.at[o], on_code(o)) for o in range(1, C)])
    near = sorted(range(1, A), key=lambda o: min(o, A - o))
    z_copies = {o: remote(items_ref, xs.at[o, 0], z_send.at[o], z_recv.at[o], on_line(o)) for o in near}
    start([z_copies[o] for o in near[:2]])
    xs[0, 0] = items_ref[...]

    for q in range(PARTS):
        loads[q].wait()

        def scale(j, _):
            at = pl.ds(pl.multiple_of(q * rows + j * LANES, LANES), LANES)
            codes = cw[at, :].T
            norm = lax.rsqrt(jnp.mean(codes * codes, axis=0, keepdims=True) + EPSILON) * (INVERSE_TEMP / D)
            high, low = split(codes * norm)
            ccat[:D, at] = high
            ccat[D:2 * D, at] = high
            ccat[2 * D:, at] = low
            return 0
        lax.fori_loop(0, rows // LANES, scale, 0)

    def pick_for(off):
        base = lax.rem(c + off, C) * R

        def one(i, _):
            index = assign_ref[base + i] - c * L
            inside = (index >= 0) & (index < L)
            row = cw[pl.ds(jnp.clip(index, 0, L - 1), 1), :]
            pick[off, pl.ds(i, 1), :] = jnp.where(inside, row, 0.0)
            return 0
        lax.fori_loop(0, R, one, 0, unroll=8)

    p_copies = [remote(pick.at[o], pickr.at[o], p_send.at[o], p_recv.at[o], on_code(o)) for o in range(1, C)]

    def prepare(slot):
        for s in range(C):
            high, low = split(unit_rows(xs[slot, s]))
            xcat[s * R:(s + 1) * R, :D] = high
            xcat[s * R:(s + 1) * R, D:2 * D] = low
            xcat[s * R:(s + 1) * R, 2 * D:] = high
            part = xs[slot, s, :, pl.ds(pl.multiple_of(line * W, LANES), W)]
            xt[:, slot * G + s * R:slot * G + (s + 1) * R] = part.T

    def similar(slot, lo, hi, own=False):
        def step(j, _):
            at = pl.ds(pl.multiple_of(j * TL, LANES), TL)
            vals = jnp.exp(dot(xcat[...], ccat[:, at], (1, 0)))
            high, low = split(vals)
            khi[slot * G:(slot + 1) * G, at] = high
            klo[slot * G:(slot + 1) * G, at] = low
            if own:
                kf[:, at] = vals
                colb[0, 0, :, at] = jnp.sum(vals, axis=0, keepdims=True)
            return 0
        lax.fori_loop(lo, hi, step, 0, unroll=4)

    wait(y_copies)
    prepare(0)
    similar(0, 0, tiles, True)

    def start_b(t):
        return start([remote(colb.at[t, 0], colb.at[t, o], b_send.at[t, o], b_recv.at[t, o], on_place(o))
                      for o in range(1, B)])

    def start_a(t):
        total = colb[t, 0]
        for o in range(1, B):
            total = total + colb[t, o]
        cola[t, 0] = total
        return start([remote(cola.at[t, 0], cola.at[t, o], a_send.at[t, o], a_recv.at[t, o], on_line(o))
                      for o in range(1, A)])

    def column_total(t):
        total = cola[t, 0]
        for o in range(1, A):
            total = total + cola[t, o]
        return total

    forwards = {}

    def forward(o):
        z_copies[o].wait()
        forwards[o] = start([remote(xs.at[o, 0], xs.at[o, s], f_send.at[o, s], f_recv.at[o, s], on_code(s))
                             for s in range(1, C)])

    def begin_block(o, lo, hi):
        if lo == 0:
            wait(forwards[o])
            prepare(o)
        similar(o, lo, hi)

    half = tiles // 2
    def pick_all():
        for o in range(C):
            pick_for(o)

    def start_far():
        start([z_copies[o] for o in near[2:]])

    def forward_far():
        for o in near[2:]:
            forward(o)
        start(p_copies)

    halves = [(lambda o=o, lo=lo: begin_block(o, lo, lo + half)) for o in near for lo in (0, half)]
    work = [[start_far, pick_all], [lambda: forward(near[0])], [lambda: forward(near[1])], halves[0:1], halves[1:2],
            [forward_far] + halves[2:3], halves[3:4], [], halves[4:5], halves[5:]]

    def background():
        if work:
            for job in work.pop(0):
                job()

    for t in range(ITERS):
        copies = start_b(t)
        background()
        wait(copies)
        copies = start_a(t)
        background()
        wait(copies)
        massb[...] = 1.0 / (C * L * column_total(t))

        def row_step(j, acc):
            at = pl.ds(pl.multiple_of(j * LANES, LANES), LANES)
            return acc + kf[:, at] * massb[:, at]
        acc = lax.fori_loop(0, L // LANES, row_step, jnp.zeros((G, LANES), F32), unroll=4)
        rowx[t, 0] = jnp.sum(acc.T, axis=0, keepdims=True)
        copies = start([remote(rowx.at[t, 0], rowx.at[t, o], r_send.at[t, o], r_recv.at[t, o], on_code(o))
                        for o in range(1, C)])
        background()
        wait(copies)
        total = rowx[t, 0]
        for o in range(1, C):
            came = rowx[t, o]
            total = total + jnp.concatenate([came[:, G - o * R:], came[:, :G - o * R]], axis=1)
        row_scale = 1.0 / (N * G * total)
        if t == ITERS - 1:
            rz[0] = row_scale
            rz_copies = start([remote(rz.at[0], rz.at[o], rz_send.at[o], rz_recv.at[o], on_line(o))
                               for o in range(1, A)])
        spread = jnp.broadcast_to(row_scale, (LANES, G)).T

        def col_step(j, _):
            at = pl.ds(pl.multiple_of(j * LANES, LANES), LANES)
            colb[t + 1, 0, :, at] = jnp.sum(kf[:, at] * spread, axis=0, keepdims=True)
            return 0
        lax.fori_loop(0, L // LANES, col_step, 0, unroll=4)

    copies = start_b(ITERS)
    while work:
        background()
    wait(rz_copies)
    for o in range(A):
        high, low = split(xt[:, o * G:(o + 1) * G] * rz[o])
        wcat[:W, o * G:(o + 1) * G] = high
        wcat[W:, o * G:(o + 1) * G] = low

    def weighted(q):
        def step(j, _):
            TN = min(Lq, 512)
            src = pl.ds(pl.multiple_of(q * Lq + j * TN, LANES), TN)
            dst = pl.ds(pl.multiple_of(j * TN, LANES), TN)
            both = dot(wcat[...], khi[:, src], (1, 0))
            vals = both[:W] + both[W:] + dot(wcat[:W, :], klo[:, src], (1, 0))
            for g in range(B):
                num[q, g % 2, g // 2, :, dst] = vals[g * d:(g + 1) * d]
            return 0
        lax.fori_loop(0, Lq // min(Lq, 512), step, 0)
        return start([remote(num.at[q, 1 - core], numc.at[q], c_send.at[q], c_recv.at[q],
                             {"dp": line * B + outer * 2 + (1 - core)})])

    def exchange(q):
        numx[q] = num[q, core] + numc[q]
        return start([remote(numx.at[q, lax.rem(outer + o, H)], numr.at[q, o], h_send.at[q, o], h_recv.at[q, o],
                             on_outer(o)) for o in range(1, H)])

    core_copies, outer_copies = [], []
    for q in range(PARTS):
        core_copies.append(weighted(q))
        if q == 0:
            wait(copies)
            copies = start_a(ITERS)
        else:
            wait(core_copies[q - 1])
            outer_copies.append(exchange(q - 1))
    wait(core_copies[PARTS - 1])
    outer_copies.append(exchange(PARTS - 1))
    wait(p_copies)
    looked = pick[0]
    for o in range(1, C):
        looked = looked + pickr[o]
    looked_ref[...] = looked
    wait(copies)
    massb[...] = 1.0 / column_total(ITERS)
    for q in range(PARTS):
        wait(outer_copies[q])
        total = numx[q, outer]
        for o in range(1, H):
            total = total + numr[q, o]
        out_ref[:, q * Lq:(q + 1) * Lq] = total * massb[:, q * Lq:(q + 1) * Lq]


def finish(total_ref, items_ref, looked_ref, out_ref, residual_ref):
    out_ref[...] = total_ref[...]
    residual_ref[...] = items_ref[...] - looked_ref[...]


def body(items, codewords, assign):
    C, N = lax.axis_size("code"), lax.axis_size("dp")
    R, D = items.shape
    L = codewords.shape[0]
    A = D // LANES
    B, G, d, H, Lq = N // A, C * R, D // N, N // A // 2, L // PARTS
    dma = pltpu.SemaphoreType.DMA
    T = ITERS + 1
    flops = 2 * 3 * A * G * L * (D + LANES)
    out, looked = pl.pallas_call(
        functools.partial(kernel, A, B, C),
        out_shape=(jax.ShapeDtypeStruct((d, L), F32), jax.ShapeDtypeStruct((R, D), F32)),
        in_specs=[pl.BlockSpec(memory_space=pltpu.VMEM), pl.BlockSpec(memory_space=pl.ANY),
                  pl.BlockSpec(memory_space=pltpu.SMEM)],
        out_specs=[pl.BlockSpec(memory_space=pltpu.VMEM)] * 2,
        scratch_shapes=[
            pltpu.VMEM((L, D), F32), pltpu.VMEM((3 * D, L), BF16),
            pltpu.VMEM((A, C, R, D), F32), pltpu.VMEM((G, 3 * D), BF16),
            pltpu.VMEM((G, L), F32), pltpu.VMEM((A * G, L), BF16), pltpu.VMEM((A * G, L), BF16),
            pltpu.VMEM((C, R, D), F32), pltpu.VMEM((C, R, D), F32),
            pltpu.VMEM((T, B, 1, L), F32), pltpu.VMEM((T, A, 1, L), F32),
            pltpu.VMEM((ITERS, C, 1, G), F32), pltpu.VMEM((A, 1, G), F32), pltpu.VMEM((1, L), F32),
            pltpu.VMEM((D // A, A * G), F32), pltpu.VMEM((2 * (D // A), A * G), BF16),
            pltpu.VMEM((PARTS, 2, H, d, Lq), F32), pltpu.VMEM((PARTS, H, d, Lq), F32),
            pltpu.VMEM((PARTS, H, d, Lq), F32), pltpu.VMEM((PARTS, H, d, Lq), F32),
            dma((PARTS,)), dma((C,)), dma((C,)), dma((A,)), dma((A,)), dma((A, C)), dma((A, C)), dma((C,)), dma((C,)),
            dma((T, B)), dma((T, B)), dma((T, A)), dma((T, A)), dma((ITERS, C)), dma((ITERS, C)),
            dma((A,)), dma((A,)), dma((PARTS,)), dma((PARTS,)), dma((PARTS, H)), dma((PARTS, H)),
        ],
        compiler_params=pltpu.CompilerParams(collective_id=0, has_side_effects=True,
                                             vmem_limit_bytes=60 * 1024 * 1024),
        cost_estimate=pl.CostEstimate(flops=flops, bytes_accessed=4 * (L * D + 4 * R * D), transcendentals=A * G * L),
        name="sinkhorn_level",
    )(items, codewords, assign)
    new_codewords, residual = pl.pallas_call(
        finish,
        out_shape=(jax.ShapeDtypeStruct((d, L), F32), jax.ShapeDtypeStruct((R, D), F32)),
        in_specs=[pl.BlockSpec(memory_space=pltpu.VMEM)] * 3,
        out_specs=[pl.BlockSpec(memory_space=pltpu.VMEM)] * 2,
        name="write_outputs",
    )(out, items, looked)
    return new_codewords.T, residual


def solution(mesh):
    in_specs = (P(("dp", "code"), None), P("code", None), P("dp"))
    out_specs = (P("code", "dp"), P(("dp", "code"), None))
    return jax.shard_map(body, mesh=mesh, in_specs=in_specs, out_specs=out_specs, check_vma=False)
```

```python
import functools

import jax
import jax.numpy as jnp
from jax import lax
from jax.experimental import pallas as pl
from jax.experimental.pallas import tpu as pltpu
from jax.sharding import PartitionSpec as P

ITERS = 3
LANES = 128
PARTS = 4
EPSILON = 1e-05
INVERSE_TEMP = 64.0
MESH = pl.DeviceIdType.MESH
F32, BF16 = jnp.float32, jnp.bfloat16


def unit_rows(values):
    return values * lax.rsqrt(jnp.mean(values * values, axis=-1, keepdims=True) + EPSILON)


def split(values):
    high = values.astype(BF16)
    return high, (values - high.astype(F32)).astype(BF16)


def dot(left, right, contract):
    return lax.dot_general(left, right, ((contract[:1], contract[1:]), ((), ())), preferred_element_type=F32)


def kernel(A, B, C, items_ref, code_ref, assign_ref, out_ref, looked_ref,
           cw, ccat, xs, xcat, kf, khi, klo, pick, pickr, colb, cola, rowx, rz, massb, xt, wcat,
           num, numc, numx, numr,
           load_sem, y_send, y_recv, z_send, z_recv, f_send, f_recv, p_send, p_recv,
           b_send, b_recv, a_send, a_recv, r_send, r_recv, rz_send, rz_recv, c_send, c_recv, h_send, h_recv):
    R, D = items_ref.shape
    L = code_ref.shape[0]
    G = C * R
    N = A * B
    H = B // 2
    d = D // N
    W = D // A
    TL = min(L, max(LANES, 65536 // G))
    tiles = L // TL
    Lq = L // PARTS
    dp, c = lax.axis_index("dp"), lax.axis_index("code")
    line, place = lax.div(dp, B), lax.rem(dp, B)
    outer, core = lax.div(place, 2), lax.rem(place, 2)

    def on_line(off):
        return {"dp": lax.rem(line + off, A) * B + place}

    def on_place(off):
        return {"dp": line * B + lax.rem(place + off, B)}

    def on_code(off):
        return {"code": lax.rem(c + off, C)}

    def on_outer(off):
        return {"dp": line * B + lax.rem(outer + off, H) * 2 + core}

    def remote(src, dst, send, recv, where):
        return pltpu.make_async_remote_copy(src_ref=src, dst_ref=dst, send_sem=send, recv_sem=recv,
                                            device_id=where, device_id_type=MESH)

    def start(copies):
        for copy in copies:
            copy.start()
        return copies

    def wait(copies):
        for copy in copies:
            copy.wait()

    rows = L // PARTS
    loads = [pltpu.make_async_copy(code_ref.at[pl.ds(q * rows, rows)], cw.at[pl.ds(q * rows, rows)], load_sem.at[q])
             for q in range(PARTS)]
    start(loads)
    barrier = pltpu.get_barrier_semaphore()
    peers = [on_line(o) for o in range(1, A)] + [on_place(o) for o in range(1, B)] + [on_code(o) for o in range(1, C)]
    for peer in peers:
        pl.semaphore_signal(barrier, inc=1, device_id=peer, device_id_type=MESH)
    pl.semaphore_wait(barrier, len(peers))

    y_copies = start([remote(items_ref, xs.at[0, o], y_send.at[o], y_recv.at[o], on_code(o)) for o in range(1, C)])
    near = sorted(range(1, A), key=lambda o: min(o, A - o))
    z_copies = {o: remote(items_ref, xs.at[o, 0], z_send.at[o], z_recv.at[o], on_line(o)) for o in near}
    start([z_copies[o] for o in near[:2]])
    xs[0, 0] = items_ref[...]

    for q in range(PARTS):
        loads[q].wait()

        def scale(j, _):
            at = pl.ds(pl.multiple_of(q * rows + j * LANES, LANES), LANES)
            codes = cw[at, :].T
            norm = lax.rsqrt(jnp.mean(codes * codes, axis=0, keepdims=True) + EPSILON) * (INVERSE_TEMP / D)
            high, low = split(codes * norm)
            ccat[:D, at] = high
            ccat[D:2 * D, at] = high
            ccat[2 * D:, at] = low
            return 0
        lax.fori_loop(0, rows // LANES, scale, 0)

    def pick_for(off):
        base = lax.rem(c + off, C) * R

        def one(i, _):
            index = assign_ref[base + i] - c * L
            inside = (index >= 0) & (index < L)
            row = cw[pl.ds(jnp.clip(index, 0, L - 1), 1), :]
            pick[off, pl.ds(i, 1), :] = jnp.where(inside, row, 0.0)
            return 0
        lax.fori_loop(0, R, one, 0, unroll=8)

    p_copies = [remote(pick.at[o], pickr.at[o], p_send.at[o], p_recv.at[o], on_code(o)) for o in range(1, C)]

    def prepare(slot):
        for s in range(C):
            high, low = split(unit_rows(xs[slot, s]))
            xcat[s * R:(s + 1) * R, :D] = high
            xcat[s * R:(s + 1) * R, D:2 * D] = low
            xcat[s * R:(s + 1) * R, 2 * D:] = high
            part = xs[slot, s, :, pl.ds(pl.multiple_of(line * W, LANES), W)]
            xt[:, slot * G + s * R:slot * G + (s + 1) * R] = part.T

    def similar(slot, lo, hi, own=False):
        def step(j, _):
            at = pl.ds(pl.multiple_of(j * TL, LANES), TL)
            vals = jnp.exp(dot(xcat[...], ccat[:, at], (1, 0)))
            high, low = split(vals)
            khi[slot * G:(slot + 1) * G, at] = high
            klo[slot * G:(slot + 1) * G, at] = low
            if own:
                kf[:, at] = vals
                colb[0, 0, :, at] = jnp.sum(vals, axis=0, keepdims=True)
            return 0
        lax.fori_loop(lo, hi, step, 0, unroll=4)

    wait(y_copies)
    prepare(0)
    similar(0, 0, tiles, True)

    def start_b(t):
        return start([remote(colb.at[t, 0], colb.at[t, o], b_send.at[t, o], b_recv.at[t, o], on_place(o))
                      for o in range(1, B)])

    def start_a(t):
        total = colb[t, 0]
        for o in range(1, B):
            total = total + colb[t, o]
        cola[t, 0] = total
        return start([remote(cola.at[t, 0], cola.at[t, o], a_send.at[t, o], a_recv.at[t, o], on_line(o))
                      for o in range(1, A)])

    def column_total(t):
        total = cola[t, 0]
        for o in range(1, A):
            total = total + cola[t, o]
        return total

    forwards = {}

    def forward(o):
        z_copies[o].wait()
        forwards[o] = start([remote(xs.at[o, 0], xs.at[o, s], f_send.at[o, s], f_recv.at[o, s], on_code(s))
                             for s in range(1, C)])

    def begin_block(o, lo, hi):
        if lo == 0:
            wait(forwards[o])
            prepare(o)
        similar(o, lo, hi)

    half = tiles // 2
    def pick_all():
        for o in range(C):
            pick_for(o)

    halves = [(lambda o=o, lo=lo: begin_block(o, lo, lo + half)) for o in near for lo in (0, half)]
    work = [[lambda: pick_for(0)], [lambda: [pick_for(o) for o in range(1, C)]], [],
            [], halves[0:1], halves[1:2], halves[2:3], halves[3:4], halves[4:5], halves[5:]]

    def background():
        if work:
            for job in work.pop(0):
                job()

    for t in range(ITERS):
        copies = start_b(t)
        background()
        wait(copies)
        copies = start_a(t)
        background()
        wait(copies)
        if t == 0:
            start([z_copies[o] for o in near[2:]])
        massb[...] = 1.0 / (C * L * column_total(t))

        def row_step(j, acc):
            at = pl.ds(pl.multiple_of(j * LANES, LANES), LANES)
            return acc + kf[:, at] * massb[:, at]
        acc = lax.fori_loop(0, L // LANES, row_step, jnp.zeros((G, LANES), F32), unroll=4)
        rowx[t, 0] = jnp.sum(acc.T, axis=0, keepdims=True)
        copies = start([remote(rowx.at[t, 0], rowx.at[t, o], r_send.at[t, o], r_recv.at[t, o], on_code(o))
                        for o in range(1, C)])
        background()
        wait(copies)
        for o in (near[:2], near[2:], ())[t]:
            forward(o)
        if t == ITERS - 1:
            start(p_copies)
        total = rowx[t, 0]
        for o in range(1, C):
            came = rowx[t, o]
            total = total + jnp.concatenate([came[:, G - o * R:], came[:, :G - o * R]], axis=1)
        row_scale = 1.0 / (N * G * total)
        if t == ITERS - 1:
            rz[0] = row_scale
            rz_copies = start([remote(rz.at[0], rz.at[o], rz_send.at[o], rz_recv.at[o], on_line(o))
                               for o in range(1, A)])
        spread = jnp.broadcast_to(row_scale, (LANES, G)).T

        def col_step(j, _):
            at = pl.ds(pl.multiple_of(j * LANES, LANES), LANES)
            colb[t + 1, 0, :, at] = jnp.sum(kf[:, at] * spread, axis=0, keepdims=True)
            return 0
        lax.fori_loop(0, L // LANES, col_step, 0, unroll=4)

    copies = start_b(ITERS)
    while work:
        background()
    wait(rz_copies)
    for o in range(A):
        high, low = split(xt[:, o * G:(o + 1) * G] * rz[o])
        wcat[:W, o * G:(o + 1) * G] = high
        wcat[W:, o * G:(o + 1) * G] = low

    def weighted(q):
        def step(j, _):
            TN = min(Lq, 512)
            src = pl.ds(pl.multiple_of(q * Lq + j * TN, LANES), TN)
            dst = pl.ds(pl.multiple_of(j * TN, LANES), TN)
            both = dot(wcat[...], khi[:, src], (1, 0))
            vals = both[:W] + both[W:] + dot(wcat[:W, :], klo[:, src], (1, 0))
            for g in range(B):
                num[q, g % 2, g // 2, :, dst] = vals[g * d:(g + 1) * d]
            return 0
        lax.fori_loop(0, Lq // min(Lq, 512), step, 0)
        return start([remote(num.at[q, 1 - core], numc.at[q], c_send.at[q], c_recv.at[q],
                             {"dp": line * B + outer * 2 + (1 - core)})])

    def exchange(q):
        numx[q] = num[q, core] + numc[q]
        return start([remote(numx.at[q, lax.rem(outer + o, H)], numr.at[q, o], h_send.at[q, o], h_recv.at[q, o],
                             on_outer(o)) for o in range(1, H)])

    core_copies, outer_copies = [], []
    for q in range(PARTS):
        core_copies.append(weighted(q))
        if q == 0:
            wait(copies)
            copies = start_a(ITERS)
        else:
            wait(core_copies[q - 1])
            outer_copies.append(exchange(q - 1))
    wait(core_copies[PARTS - 1])
    outer_copies.append(exchange(PARTS - 1))
    wait(p_copies)
    looked = pick[0]
    for o in range(1, C):
        looked = looked + pickr[o]
    looked_ref[...] = looked
    wait(copies)
    massb[...] = 1.0 / column_total(ITERS)
    for q in range(PARTS):
        wait(outer_copies[q])
        total = numx[q, outer]
        for o in range(1, H):
            total = total + numr[q, o]
        out_ref[:, q * Lq:(q + 1) * Lq] = total * massb[:, q * Lq:(q + 1) * Lq]


def finish(total_ref, items_ref, looked_ref, out_ref, residual_ref):
    out_ref[...] = total_ref[...]
    residual_ref[...] = items_ref[...] - looked_ref[...]


def body(items, codewords, assign):
    C, N = lax.axis_size("code"), lax.axis_size("dp")
    R, D = items.shape
    L = codewords.shape[0]
    A = D // LANES
    B, G, d, H, Lq = N // A, C * R, D // N, N // A // 2, L // PARTS
    dma = pltpu.SemaphoreType.DMA
    T = ITERS + 1
    flops = 2 * 3 * A * G * L * (D + LANES)
    out, looked = pl.pallas_call(
        functools.partial(kernel, A, B, C),
        out_shape=(jax.ShapeDtypeStruct((d, L), F32), jax.ShapeDtypeStruct((R, D), F32)),
        in_specs=[pl.BlockSpec(memory_space=pltpu.VMEM), pl.BlockSpec(memory_space=pl.ANY),
                  pl.BlockSpec(memory_space=pltpu.SMEM)],
        out_specs=[pl.BlockSpec(memory_space=pltpu.VMEM)] * 2,
        scratch_shapes=[
            pltpu.VMEM((L, D), F32), pltpu.VMEM((3 * D, L), BF16),
            pltpu.VMEM((A, C, R, D), F32), pltpu.VMEM((G, 3 * D), BF16),
            pltpu.VMEM((G, L), F32), pltpu.VMEM((A * G, L), BF16), pltpu.VMEM((A * G, L), BF16),
            pltpu.VMEM((C, R, D), F32), pltpu.VMEM((C, R, D), F32),
            pltpu.VMEM((T, B, 1, L), F32), pltpu.VMEM((T, A, 1, L), F32),
            pltpu.VMEM((ITERS, C, 1, G), F32), pltpu.VMEM((A, 1, G), F32), pltpu.VMEM((1, L), F32),
            pltpu.VMEM((D // A, A * G), F32), pltpu.VMEM((2 * (D // A), A * G), BF16),
            pltpu.VMEM((PARTS, 2, H, d, Lq), F32), pltpu.VMEM((PARTS, H, d, Lq), F32),
            pltpu.VMEM((PARTS, H, d, Lq), F32), pltpu.VMEM((PARTS, H, d, Lq), F32),
            dma((PARTS,)), dma((C,)), dma((C,)), dma((A,)), dma((A,)), dma((A, C)), dma((A, C)), dma((C,)), dma((C,)),
            dma((T, B)), dma((T, B)), dma((T, A)), dma((T, A)), dma((ITERS, C)), dma((ITERS, C)),
            dma((A,)), dma((A,)), dma((PARTS,)), dma((PARTS,)), dma((PARTS, H)), dma((PARTS, H)),
        ],
        compiler_params=pltpu.CompilerParams(collective_id=0, has_side_effects=True,
                                             vmem_limit_bytes=60 * 1024 * 1024),
        cost_estimate=pl.CostEstimate(flops=flops, bytes_accessed=4 * (L * D + 4 * R * D), transcendentals=A * G * L),
        name="sinkhorn_level",
    )(items, codewords, assign)
    new_codewords, residual = pl.pallas_call(
        finish,
        out_shape=(jax.ShapeDtypeStruct((d, L), F32), jax.ShapeDtypeStruct((R, D), F32)),
        in_specs=[pl.BlockSpec(memory_space=pltpu.VMEM)] * 3,
        out_specs=[pl.BlockSpec(memory_space=pltpu.VMEM)] * 2,
        name="write_outputs",
    )(out, items, looked)
    return new_codewords.T, residual


def solution(mesh):
    in_specs = (P(("dp", "code"), None), P("code", None), P("dp"))
    out_specs = (P("code", "dp"), P(("dp", "code"), None))
    return jax.shard_map(body, mesh=mesh, in_specs=in_specs, out_specs=out_specs, check_vma=False)
```

```python
import functools

import jax
import jax.numpy as jnp
from jax import lax
from jax.experimental import pallas as pl
from jax.experimental.pallas import tpu as pltpu
from jax.sharding import PartitionSpec as P

ITERS = 3
LANES = 128
PARTS = 8
EPSILON = 1e-05
INVERSE_TEMP = 64.0
MESH = pl.DeviceIdType.MESH
F32, BF16 = jnp.float32, jnp.bfloat16


def unit_rows(values):
    return values * lax.rsqrt(jnp.mean(values * values, axis=-1, keepdims=True) + EPSILON)


def split(values):
    high = values.astype(BF16)
    return high, (values - high.astype(F32)).astype(BF16)


def dot(left, right, contract):
    return lax.dot_general(left, right, ((contract[:1], contract[1:]), ((), ())), preferred_element_type=F32)


def kernel(A, B, C, items_ref, code_ref, assign_ref, out_ref, looked_ref,
           cw, ccat, xs, xcat, kf, khi, klo, pick, pickr, colb, cola, rowx, rz, massb, xt, wcat,
           num, numc, numx, numr,
           load_sem, y_send, y_recv, z_send, z_recv, f_send, f_recv, p_send, p_recv,
           b_send, b_recv, a_send, a_recv, r_send, r_recv, rz_send, rz_recv, c_send, c_recv, h_send, h_recv):
    R, D = items_ref.shape
    L = code_ref.shape[0]
    G = C * R
    N = A * B
    H = B // 2
    d = D // N
    W = D // A
    TL = min(L, max(LANES, 65536 // G))
    tiles = L // TL
    Lq = L // PARTS
    dp, c = lax.axis_index("dp"), lax.axis_index("code")
    line, place = lax.div(dp, B), lax.rem(dp, B)
    outer, core = lax.div(place, 2), lax.rem(place, 2)

    def on_line(off):
        return {"dp": lax.rem(line + off, A) * B + place}

    def on_place(off):
        return {"dp": line * B + lax.rem(place + off, B)}

    def on_code(off):
        return {"code": lax.rem(c + off, C)}

    def on_outer(off):
        return {"dp": line * B + lax.rem(outer + off, H) * 2 + core}

    def remote(src, dst, send, recv, where):
        return pltpu.make_async_remote_copy(src_ref=src, dst_ref=dst, send_sem=send, recv_sem=recv,
                                            device_id=where, device_id_type=MESH)

    def start(copies):
        for copy in copies:
            copy.start()
        return copies

    def wait(copies):
        for copy in copies:
            copy.wait()

    rows = L // PARTS
    loads = [pltpu.make_async_copy(code_ref.at[pl.ds(q * rows, rows)], cw.at[pl.ds(q * rows, rows)], load_sem.at[q])
             for q in range(PARTS)]
    start(loads)
    barrier = pltpu.get_barrier_semaphore()
    peers = [on_line(o) for o in range(1, A)] + [on_place(o) for o in range(1, B)] + [on_code(o) for o in range(1, C)]
    for peer in peers:
        pl.semaphore_signal(barrier, inc=1, device_id=peer, device_id_type=MESH)
    pl.semaphore_wait(barrier, len(peers))

    y_copies = start([remote(items_ref, xs.at[0, o], y_send.at[o], y_recv.at[o], on_code(o)) for o in range(1, C)])
    near = sorted(range(1, A), key=lambda o: min(o, A - o))
    z_copies = {o: remote(items_ref, xs.at[o, 0], z_send.at[o], z_recv.at[o], on_line(o)) for o in near}
    start([z_copies[near[0]]])
    xs[0, 0] = items_ref[...]

    for q in range(PARTS):
        loads[q].wait()

        def scale(j, _):
            at = pl.ds(pl.multiple_of(q * rows + j * LANES, LANES), LANES)
            codes = cw[at, :].T
            norm = lax.rsqrt(jnp.mean(codes * codes, axis=0, keepdims=True) + EPSILON) * (INVERSE_TEMP / D)
            high, low = split(codes * norm)
            ccat[:D, at] = high
            ccat[D:2 * D, at] = high
            ccat[2 * D:, at] = low
            return 0
        lax.fori_loop(0, rows // LANES, scale, 0)

    start([z_copies[o] for o in near[1:2]])

    def pick_for(off):
        base = lax.rem(c + off, C) * R

        def one(i, _):
            index = assign_ref[base + i] - c * L
            inside = (index >= 0) & (index < L)
            row = cw[pl.ds(jnp.clip(index, 0, L - 1), 1), :]
            pick[off, pl.ds(i, 1), :] = jnp.where(inside, row, 0.0)
            return 0
        lax.fori_loop(0, R, one, 0, unroll=8)

    p_copies = [remote(pick.at[o], pickr.at[o], p_send.at[o], p_recv.at[o], on_code(o)) for o in range(1, C)]

    def prepare(slot):
        for s in range(C):
            high, low = split(unit_rows(xs[slot, s]))
            xcat[s * R:(s + 1) * R, :D] = high
            xcat[s * R:(s + 1) * R, D:2 * D] = low
            xcat[s * R:(s + 1) * R, 2 * D:] = high
            part = xs[slot, s, :, pl.ds(pl.multiple_of(line * W, LANES), W)]
            xt[:, slot * G + s * R:slot * G + (s + 1) * R] = part.T

    def similar(slot, lo, hi, own=False):
        def step(j, _):
            at = pl.ds(pl.multiple_of(j * TL, LANES), TL)
            vals = jnp.exp(dot(xcat[...], ccat[:, at], (1, 0)))
            high, low = split(vals)
            khi[slot * G:(slot + 1) * G, at] = high
            klo[slot * G:(slot + 1) * G, at] = low
            if own:
                kf[:, at] = vals
                colb[0, 0, :, at] = jnp.sum(vals, axis=0, keepdims=True)
            return 0
        lax.fori_loop(lo, hi, step, 0, unroll=4)

    forwards = {}

    def forward(o):
        z_copies[o].wait()
        forwards[o] = start([remote(xs.at[o, 0], xs.at[o, s], f_send.at[o, s], f_recv.at[o, s], on_code(s))
                             for s in range(1, C)])

    wait(y_copies)
    forward(near[0])
    prepare(0)
    similar(0, 0, tiles, True)

    def start_b(t):
        return start([remote(colb.at[t, 0], colb.at[t, o], b_send.at[t, o], b_recv.at[t, o], on_place(o))
                      for o in range(1, B)])

    def start_a(t):
        total = colb[t, 0]
        for o in range(1, B):
            total = total + colb[t, o]
        cola[t, 0] = total
        return start([remote(cola.at[t, 0], cola.at[t, o], a_send.at[t, o], a_recv.at[t, o], on_line(o))
                      for o in range(1, A)])

    def column_total(t):
        total = cola[t, 0]
        for o in range(1, A):
            total = total + cola[t, o]
        return total

    def begin_block(o, lo, hi):
        if lo == 0:
            wait(forwards[o])
            prepare(o)
        similar(o, lo, hi)

    half = tiles // 2
    halves = [(lambda o=o, lo=lo: begin_block(o, lo, lo + half)) for o in near for lo in (0, half)]
    work = [[lambda: pick_for(0)], [lambda: [pick_for(o) for o in range(1, C)]], halves[0:1],
            halves[1:2], halves[2:3], halves[3:4], [], halves[4:5], halves[5:], []]

    def background():
        if work:
            for job in work.pop(0):
                job()

    for t in range(ITERS):
        copies = start_b(t)
        if t == 0:
            for o in near[1:2]:
                forward(o)
        background()
        wait(copies)
        copies = start_a(t)
        background()
        wait(copies)
        if t == 0:
            start([z_copies[o] for o in near[2:]])
        massb[...] = 1.0 / (C * L * column_total(t))

        def row_step(j, acc):
            at = pl.ds(pl.multiple_of(j * LANES, LANES), LANES)
            return acc + kf[:, at] * massb[:, at]
        acc = lax.fori_loop(0, L // LANES, row_step, jnp.zeros((G, LANES), F32), unroll=4)
        rowx[t, 0] = jnp.sum(acc.T, axis=0, keepdims=True)
        copies = start([remote(rowx.at[t, 0], rowx.at[t, o], r_send.at[t, o], r_recv.at[t, o], on_code(o))
                        for o in range(1, C)])
        background()
        wait(copies)
        if t == 1:
            for o in near[2:]:
                forward(o)
        if t == ITERS - 1:
            start(p_copies)
        total = rowx[t, 0]
        for o in range(1, C):
            came = rowx[t, o]
            total = total + jnp.concatenate([came[:, G - o * R:], came[:, :G - o * R]], axis=1)
        row_scale = 1.0 / (N * G * total)
        if t == ITERS - 1:
            rz[0] = row_scale
            rz_copies = start([remote(rz.at[0], rz.at[o], rz_send.at[o], rz_recv.at[o], on_line(o))
                               for o in range(1, A)])
        spread = jnp.broadcast_to(row_scale, (LANES, G)).T

        def col_step(j, _):
            at = pl.ds(pl.multiple_of(j * LANES, LANES), LANES)
            colb[t + 1, 0, :, at] = jnp.sum(kf[:, at] * spread, axis=0, keepdims=True)
            return 0
        lax.fori_loop(0, L // LANES, col_step, 0, unroll=4)

    copies = start_b(ITERS)
    while work:
        background()
    wait(rz_copies)
    for o in range(A):
        high, low = split(xt[:, o * G:(o + 1) * G] * rz[o])
        wcat[:W, o * G:(o + 1) * G] = high
        wcat[W:, o * G:(o + 1) * G] = low

    def weighted(q):
        def step(j, _):
            TN = min(Lq, 512)
            src = pl.ds(pl.multiple_of(q * Lq + j * TN, LANES), TN)
            dst = pl.ds(pl.multiple_of(j * TN, LANES), TN)
            both = dot(wcat[...], khi[:, src], (1, 0))
            vals = both[:W] + both[W:] + dot(wcat[:W, :], klo[:, src], (1, 0))
            for g in range(B):
                num[q, g % 2, g // 2, :, dst] = vals[g * d:(g + 1) * d]
            return 0
        lax.fori_loop(0, Lq // min(Lq, 512), step, 0)
        return start([remote(num.at[q, 1 - core], numc.at[q], c_send.at[q], c_recv.at[q],
                             {"dp": line * B + outer * 2 + (1 - core)})])

    def exchange(q):
        numx[q] = num[q, core] + numc[q]
        return start([remote(numx.at[q, lax.rem(outer + o, H)], numr.at[q, o], h_send.at[q, o], h_recv.at[q, o],
                             on_outer(o)) for o in range(1, H)])

    core_copies, outer_copies = [], []
    for q in range(PARTS):
        core_copies.append(weighted(q))
        if q == 0:
            wait(copies)
            copies = start_a(ITERS)
        else:
            wait(core_copies[q - 1])
            outer_copies.append(exchange(q - 1))
    wait(core_copies[PARTS - 1])
    outer_copies.append(exchange(PARTS - 1))
    wait(p_copies)
    looked = pick[0]
    for o in range(1, C):
        looked = looked + pickr[o]
    looked_ref[...] = looked
    wait(copies)
    massb[...] = 1.0 / column_total(ITERS)
    for q in range(PARTS):
        wait(outer_copies[q])
        total = numx[q, outer]
        for o in range(1, H):
            total = total + numr[q, o]
        out_ref[:, q * Lq:(q + 1) * Lq] = total * massb[:, q * Lq:(q + 1) * Lq]


def finish(total_ref, items_ref, looked_ref, out_ref, residual_ref):
    out_ref[...] = total_ref[...]
    residual_ref[...] = items_ref[...] - looked_ref[...]


def body(items, codewords, assign):
    C, N = lax.axis_size("code"), lax.axis_size("dp")
    R, D = items.shape
    L = codewords.shape[0]
    A = D // LANES
    B, G, d, H, Lq = N // A, C * R, D // N, N // A // 2, L // PARTS
    dma = pltpu.SemaphoreType.DMA
    T = ITERS + 1
    flops = 2 * 3 * A * G * L * (D + LANES)
    out, looked = pl.pallas_call(
        functools.partial(kernel, A, B, C),
        out_shape=(jax.ShapeDtypeStruct((d, L), F32), jax.ShapeDtypeStruct((R, D), F32)),
        in_specs=[pl.BlockSpec(memory_space=pltpu.VMEM), pl.BlockSpec(memory_space=pl.ANY),
                  pl.BlockSpec(memory_space=pltpu.SMEM)],
        out_specs=[pl.BlockSpec(memory_space=pltpu.VMEM)] * 2,
        scratch_shapes=[
            pltpu.VMEM((L, D), F32), pltpu.VMEM((3 * D, L), BF16),
            pltpu.VMEM((A, C, R, D), F32), pltpu.VMEM((G, 3 * D), BF16),
            pltpu.VMEM((G, L), F32), pltpu.VMEM((A * G, L), BF16), pltpu.VMEM((A * G, L), BF16),
            pltpu.VMEM((C, R, D), F32), pltpu.VMEM((C, R, D), F32),
            pltpu.VMEM((T, B, 1, L), F32), pltpu.VMEM((T, A, 1, L), F32),
            pltpu.VMEM((ITERS, C, 1, G), F32), pltpu.VMEM((A, 1, G), F32), pltpu.VMEM((1, L), F32),
            pltpu.VMEM((D // A, A * G), F32), pltpu.VMEM((2 * (D // A), A * G), BF16),
            pltpu.VMEM((PARTS, 2, H, d, Lq), F32), pltpu.VMEM((PARTS, H, d, Lq), F32),
            pltpu.VMEM((PARTS, H, d, Lq), F32), pltpu.VMEM((PARTS, H, d, Lq), F32),
            dma((PARTS,)), dma((C,)), dma((C,)), dma((A,)), dma((A,)), dma((A, C)), dma((A, C)), dma((C,)), dma((C,)),
            dma((T, B)), dma((T, B)), dma((T, A)), dma((T, A)), dma((ITERS, C)), dma((ITERS, C)),
            dma((A,)), dma((A,)), dma((PARTS,)), dma((PARTS,)), dma((PARTS, H)), dma((PARTS, H)),
        ],
        compiler_params=pltpu.CompilerParams(collective_id=0, has_side_effects=True,
                                             vmem_limit_bytes=60 * 1024 * 1024),
        cost_estimate=pl.CostEstimate(flops=flops, bytes_accessed=4 * (L * D + 4 * R * D), transcendentals=A * G * L),
        name="sinkhorn_level",
    )(items, codewords, assign)
    new_codewords, residual = pl.pallas_call(
        finish,
        out_shape=(jax.ShapeDtypeStruct((d, L), F32), jax.ShapeDtypeStruct((R, D), F32)),
        in_specs=[pl.BlockSpec(memory_space=pltpu.VMEM)] * 3,
        out_specs=[pl.BlockSpec(memory_space=pltpu.VMEM)] * 2,
        name="write_outputs",
    )(out, items, looked)
    return new_codewords.T, residual


def solution(mesh):
    in_specs = (P(("dp", "code"), None), P("code", None), P("dp"))
    out_specs = (P("code", "dp"), P(("dp", "code"), None))
    return jax.shard_map(body, mesh=mesh, in_specs=in_specs, out_specs=out_specs, check_vma=False)
```
